32 devices in a mesh: groups: 2 (over x), kvp: 16 (over z, y, core).
Axes of the slice: x: 2, y: 2, z: 4, core: 2. Of those that a mesh axis runs over, the one named last changes fastest.
Arguments:
- queries: bfloat16 [512, 4096], P(('groups', 'kvp')), parts along dimension 0, may hold values from -8 to 8
- rotated_span_keys: bfloat16 [512, 512], P(('groups', 'kvp')), parts along dimension 0, may hold values from -8 to 8
- incoming_values: bfloat16 [512, 512], P(('groups', 'kvp')), parts along dimension 0, may hold values from -6 to 6
- stored_keys: bfloat16 [32768, 512], P(('groups', 'kvp')), parts along dimension 0, may hold values from -8 to 8
- stored_values: bfloat16 [32768, 512], P(('groups', 'kvp')), parts along dimension 0, may hold values from -6 to 6
- shard_lens: int32 [32], P('groups'), parts along dimension 0, may hold values from 1 to 1024, 12288 in all
- span_starts: int32 [4], P('groups'), parts along dimension 0, may hold values from 6144 to 12288
Outputs:
- attended: bfloat16 [512, 4096], P(('groups', 'kvp')), parts along dimension 0
The draws below stay inside these ranges and needn't reach their ends.
There are 2 independent parts, one for each index of `groups`. The reference program is written for one: setup_inputs(seed, part) draws one part's arguments, and reference() takes and returns one part's arrays. A program takes and returns all parts, laid end to end along the dimension named above; each array names one. Nothing has to cross between parts.
Inputs may be any that keep to these rules, and one draw needn't show every extreme that they name: `shard_lens`: the lengths of the 16 shards sum to 12288; one shard is full.
All inputs are finite; a program needn't handle non-finite values.
Results may differ from the reference program's by a relative error of at most 0.0023.
Values may be sent and summed in bfloat16 or wider, within the bound.
A program may use at most 64 MiB of HBM per device.

```python
import math
import jax
import jax.numpy as jnp
import numpy as np
from jax import lax

QUERY_HEADS = 32
KEY_VALUE_HEADS = 4
HEAD_SIZE = 128
SPAN = 128
SPANS = 2
SPAN_TOKENS = 256
DEVICE_SLOTS = 1024
CACHE_SLOTS_ALL = 16384
CACHED = 12288
N_KVP = 16


def draw_queries(key, part):
    vector_width = QUERY_HEADS * HEAD_SIZE
    values = jnp.clip(1.75 * jax.random.normal(jax.random.fold_in(key, 3), (SPAN_TOKENS, vector_width), jnp.float32), -8.0, 8.0)
    return values.astype(jnp.bfloat16)


def draw_stored_keys(key, part):
    vector_width = KEY_VALUE_HEADS * HEAD_SIZE
    values = jnp.clip(1.75 * jax.random.normal(jax.random.fold_in(key, 6), (CACHE_SLOTS_ALL, vector_width), jnp.float32), -8.0, 8.0)
    return values.astype(jnp.bfloat16)


def block_scale(rng, shape, pieces, smallest, top_value):
    level, own = 1.0, jax.random.fold_in(rng, 6)
    for axis_at, shards_of in pieces:
        steps = jnp.exp(jax.random.uniform(jax.random.fold_in(own, axis_at), (shards_of,), jnp.float32, smallest / len(pieces), top_value / len(pieces)))
        level = level * jnp.repeat(steps, shape[axis_at] // shards_of).reshape([-1 if axis == axis_at else 1 for axis in range(len(shape))])
    return level


def profile(count, total, limit, skew):
    weights = [(1 << 20) // math.isqrt(rank ** skew) + 1 for rank in range(2, count + 1)]
    rest, counts = total - limit - (count - 1), [1] * (count - 1)
    while rest > 0:
        free = [i for i in range(count - 1) if counts[i] < limit]
        whole, budget = sum([weights[i] for i in free]), rest
        for i in free:
            extra = min(limit - counts[i], max(1, budget * weights[i] // whole), rest)
            counts[i] = counts[i] + extra
            rest = rest - extra
    return np.array([limit] + counts)


def ragged_sizes(rng, count, total, most, slope):
    if count == 2:
        one = jax.random.randint(rng, (), max(1, total - most), min(most, total - 1) + 1)
        return jnp.stack([one, total - one])
    sizes = jnp.asarray(profile(count, total, most, slope), jnp.int32)
    twos = (count - 1) // 2
    source_of, receiver = sizes[1:1 + 2 * twos:2], sizes[2:2 + 2 * twos:2]
    room = jnp.minimum(source_of - 1, most - receiver)
    shifted = jax.random.randint(jax.random.fold_in(rng, 1), (twos,), 0, 1 << 20) % (room + 1)
    sizes = sizes.at[1:1 + 2 * twos:2].set(source_of - shifted).at[2:2 + 2 * twos:2].set(receiver + shifted)
    return sizes[jax.random.permutation(jax.random.fold_in(rng, 2), count)]


def bell_draw(own_key, dims, width, reach, pieces=(), kind=jnp.bfloat16):
    values = jax.random.normal(own_key, dims, jnp.float32) * width
    if len(pieces) > 0:
        values = block_scale(own_key, dims, pieces, -0.22, 0.18) * values
    return jnp.clip(values, min=-reach, max=reach).astype(kind)


def setup_inputs(seed: int = 0, part: int = 0) -> dict:
    arg_keys = jax.random.split(jax.random.key(seed), 8)
    own_keys = jax.random.split(jax.random.fold_in(arg_keys[7], part), 8)
    queries = draw_queries(jax.random.fold_in(jax.random.fold_in(arg_keys[7], part), 71), part)
    rotated_span_keys = bell_draw(own_keys[1], (SPAN_TOKENS, KEY_VALUE_HEADS * HEAD_SIZE), 2.4, 8.0, ((0, 16),))
    incoming_values = bell_draw(own_keys[2], (SPAN_TOKENS, KEY_VALUE_HEADS * HEAD_SIZE), 1.0, 6.0, ((0, 16),))
    stored_keys = draw_stored_keys(jax.random.fold_in(jax.random.fold_in(arg_keys[7], part), 71), part)
    stored_values = bell_draw(own_keys[4], (CACHE_SLOTS_ALL, KEY_VALUE_HEADS * HEAD_SIZE), 1.0, 6.0, ((0, 16),))
    shard_lens = ragged_sizes(own_keys[5], N_KVP, CACHED, DEVICE_SLOTS, 2).astype(jnp.int32)
    span_starts = jax.random.randint(own_keys[6], (SPANS,), CACHED // 2, CACHED + 1).astype(jnp.int32)
    return {"queries": queries, "rotated_span_keys": rotated_span_keys, "incoming_values": incoming_values, "stored_keys": stored_keys, "stored_values": stored_values, "shard_lens": shard_lens, "span_starts": span_starts}


NEG_LARGE = -1.0e30


def reference(queries, rotated_span_keys, incoming_values, stored_keys, stored_values, shard_lens, span_starts):
    query_group_size = QUERY_HEADS // KEY_VALUE_HEADS
    scale = HEAD_SIZE ** -0.5
    offsets = jnp.cumsum(shard_lens) - shard_lens
    slot_index = jnp.arange(DEVICE_SLOTS, dtype=jnp.int32)
    positions = offsets[:, None] + slot_index[None, :]
    live_slots = slot_index[None, :] < shard_lens[:, None]
    gathered_keys = stored_keys.astype(jnp.float32).reshape(N_KVP, DEVICE_SLOTS, KEY_VALUE_HEADS, HEAD_SIZE)
    gathered_values = stored_values.astype(jnp.float32).reshape(N_KVP, DEVICE_SLOTS, KEY_VALUE_HEADS, HEAD_SIZE)
    span_key_rows = rotated_span_keys.astype(jnp.float32).reshape(SPAN_TOKENS, KEY_VALUE_HEADS, HEAD_SIZE)
    span_value_rows = incoming_values.astype(jnp.float32).reshape(SPAN_TOKENS, KEY_VALUE_HEADS, HEAD_SIZE)
    gathered_query = queries.astype(jnp.float32).reshape(SPAN_TOKENS, KEY_VALUE_HEADS, query_group_size, HEAD_SIZE)
    block_row_range = 4
    key_ids = jnp.arange(SPAN_TOKENS, dtype=jnp.int32)

    def one_block(first):
        row_ids = first + jnp.arange(block_row_range, dtype=jnp.int32)
        rows_here = lax.dynamic_slice_in_dim(gathered_query, first, block_row_range, 0)
        limits = span_starts[row_ids // SPAN]
        visible = live_slots[None] & (positions[None] < limits[:, None, None])
        scores = jnp.einsum("rhgd,skhd->rhgsk", rows_here, gathered_keys) * scale
        visible_mask = visible[:, None, None]
        shard_max = jnp.max(jnp.where(visible_mask, scores, NEG_LARGE), axis=-1)
        weights = jnp.where(visible_mask, jnp.exp(scores - shard_max[..., None]), 0.0)
        shard_total = jnp.sum(weights, axis=-1)
        rounded = lax.optimization_barrier(weights.astype(jnp.bfloat16)).astype(jnp.float32)
        shard_num = jnp.einsum("rhgsk,skhd->rhgsd", rounded, gathered_values)
        span_visible = (key_ids[None, :] // SPAN == row_ids[:, None] // SPAN) & (key_ids[None, :] <= row_ids[:, None])
        span_scores = jnp.einsum("rhgd,jhd->rhgj", rows_here, span_key_rows) * scale
        span_mask = span_visible[:, None, None]
        span_max = jnp.max(jnp.where(span_mask, span_scores, NEG_LARGE), axis=-1)
        span_weights = jnp.where(span_mask, jnp.exp(span_scores - span_max[..., None]), 0.0)
        span_total = jnp.sum(span_weights, axis=-1)
        span_rounded = lax.optimization_barrier(span_weights.astype(jnp.bfloat16)).astype(jnp.float32)
        span_num = jnp.einsum("rhgj,jhd->rhgd", span_rounded, span_value_rows)
        overall = jnp.maximum(jnp.max(shard_max, axis=-1), span_max)
        shard_factor = jnp.exp(shard_max - overall[..., None])
        span_factor = jnp.exp(span_max - overall)
        numerator = jnp.sum(shard_num * shard_factor[..., None], axis=3) + span_num * span_factor[..., None]
        denominator = jnp.sum(shard_total * shard_factor, axis=-1) + span_total * span_factor
        return (numerator / denominator[..., None]).reshape(block_row_range, QUERY_HEADS * HEAD_SIZE).astype(jnp.bfloat16)

    block_starts = jnp.arange(SPAN_TOKENS // block_row_range, dtype=jnp.int32) * block_row_range
    result = lax.map(one_block, block_starts)
    return result.reshape(SPAN_TOKENS, QUERY_HEADS * HEAD_SIZE)
```

```python
import functools

import jax
import jax.numpy as jnp
from jax import lax
from jax.experimental import pallas as pl
from jax.experimental.pallas import tpu as pltpu
from jax.sharding import PartitionSpec as P

QUERY_HEADS = 32
HEADS = 4
GROUP = QUERY_HEADS // HEADS
HEAD_SIZE = 128
SPAN = 128
SPANS = 2
NEG = -1e30
SCALE2 = HEAD_SIZE ** (-0.5) * 1.4426950408889634
F32 = jnp.float32
BF16 = jnp.bfloat16
MESH = pl.DeviceIdType.MESH


def log2(x):
    return x.bit_length() - 1


def weigh(scores, visible):
    masked = jnp.where(visible, scores, NEG)
    top = jnp.max(masked, axis=0, keepdims=True)
    weights = jnp.exp2(masked * SCALE2 - top * SCALE2)
    return weights.astype(BF16), top * SCALE2, jnp.sum(weights, axis=0, keepdims=True)


def dot_nt(a, b):
    return lax.dot_general(a, b, (((1,), (1,)), ((), ())), preferred_element_type=F32)


def dot_nn(a, b):
    return lax.dot_general(a, b, (((1,), (0,)), ((), ())), preferred_element_type=F32)


def merge(one, two):
    num1, top1, sum1 = one
    num2, top2, sum2 = two
    top = jnp.maximum(top1, top2)
    f1, f2 = jnp.exp2(top1 - top), jnp.exp2(top2 - top)
    return num1 * f1 + num2 * f2, top, sum1 * f1 + sum2 * f2


def kernel(
    n, rows, pad, tile,
    counts, q_in, s_in, k_in, v_in, out,
    qbuf, sbuf, kbuf, vbuf, vt, svt, acc, rbuf, obuf,
    q_send, q_recv, s_send, s_recv, k_send, k_recv, v_send, v_recv, a_send, a_recv, o_send, o_recv,
):
    group = lax.axis_index("groups")
    me = lax.axis_index("kvp")
    head = lax.rem(me, HEADS)
    quad = lax.div(me, HEADS)
    quads = n // HEADS
    block = GROUP * rows
    per_quad = HEADS * block
    tiles = per_quad // tile
    slots = kbuf.shape[1]

    barrier = pltpu.get_barrier_semaphore()

    def greet(k, c):
        pl.semaphore_signal(barrier, inc=1, device_id=(group, lax.rem(me + k, n)), device_id_type=MESH)
        return c

    lax.fori_loop(1, n, greet, 0)
    pl.semaphore_wait(barrier, n - 1)

    def q_copy(k):
        to = lax.rem(me + k, n)
        return pltpu.make_async_remote_copy(
            src_ref=q_in.at[lax.rem(to, HEADS)],
            dst_ref=qbuf.at[pl.ds(pl.multiple_of(me * block, block), block)],
            send_sem=q_send.at[k], recv_sem=q_recv.at[k],
            device_id=(group, to), device_id_type=MESH,
        )

    def s_copy(k):
        to = lax.rem(me + k, n)
        return pltpu.make_async_remote_copy(
            src_ref=s_in.at[lax.rem(to, HEADS)],
            dst_ref=sbuf.at[:, pl.ds(pl.multiple_of(me * pad, pad), pad)],
            send_sem=s_send.at[k], recv_sem=s_recv.at[k],
            device_id=(group, to), device_id_type=MESH,
        )

    partner = head + 1 - 2 * lax.rem(head, 2)
    order = (head, partner, lax.rem(head + 2, HEADS), lax.rem(partner + 2, HEADS))

    def kv_copies(i):
        columns = pl.ds(pl.multiple_of(order[i] * HEAD_SIZE, HEAD_SIZE), HEAD_SIZE)
        if i == 0:
            return (
                pltpu.make_async_copy(k_in.at[:, columns], kbuf.at[0], k_recv.at[0]),
                pltpu.make_async_copy(v_in.at[:, columns], vbuf.at[0], v_recv.at[0]),
            )
        return tuple(
            pltpu.make_async_remote_copy(
                src_ref=src.at[:, columns], dst_ref=dst.at[i],
                send_sem=send.at[i], recv_sem=recv.at[i],
                device_id=(group, quad * HEADS + order[i]), device_id_type=MESH,
            )
            for src, dst, send, recv in ((k_in, kbuf, k_send, k_recv), (v_in, vbuf, v_send, v_recv))
        )

    kv = [kv_copies(i) for i in range(HEADS)]

    def send_q(k, c):
        q_copy(k).start()
        return c

    lax.fori_loop(1, n, send_q, 0)
    for i in range(HEADS):
        for copy in kv[i]:
            copy.start()

    def send_s(k, c):
        s_copy(k).start()
        return c

    lax.fori_loop(1, n, send_s, 0)
    qbuf[pl.ds(pl.multiple_of(me * block, block), block), :] = q_in[head]
    sbuf[:, pl.ds(pl.multiple_of(me * pad, pad), pad), :] = s_in[head]

    def wait_q(k, c):
        q_copy(k).wait_recv()
        return c

    lax.fori_loop(1, n, wait_q, 0)

    def wait_kv(i):
        for copy in kv[i]:
            if i == 0:
                copy.wait()
            else:
                copy.wait_recv()
        vt[i] = jnp.transpose(vbuf[i])

    slot_ids = lax.broadcasted_iota(jnp.int32, (slots, tile), 0)
    stat_ids = lax.broadcasted_iota(jnp.int32, (8, tile), 0)

    def queries_of(b):
        return qbuf[pl.ds(pl.multiple_of(b * tile, tile), tile), :]

    def part(i, b):
        count = counts[quad * HEADS + order[i], lax.div(b * tile, GROUP * SPAN)]
        weights, top, total = weigh(dot_nt(kbuf[i], queries_of(b)), slot_ids < count)
        return dot_nn(vt[i], weights), top, total

    def load(ref, *at):
        return (
            ref[(*at, slice(0, HEAD_SIZE))],
            ref[(*at, slice(HEAD_SIZE, HEAD_SIZE + 1))],
            ref[(*at, slice(HEAD_SIZE + 4, HEAD_SIZE + 5))],
        )

    def store(b, state):
        num, top, total = state
        acc[b, 0:HEAD_SIZE] = num
        acc[b, HEAD_SIZE : HEAD_SIZE + 8] = jnp.where(stat_ids < 4, top, total)

    wait_kv(0)

    def first(b, c):
        store(b, part(0, b))
        return c

    lax.fori_loop(0, quads * tiles, first, 0)
    wait_kv(1)

    def second(b, c):
        store(b, merge(load(acc, b), part(1, b)))
        return c

    lax.fori_loop(0, quads * tiles, second, 0)
    wait_kv(2)
    wait_kv(3)

    def a_copy(k):
        to = lax.rem(quad + k, quads)
        return pltpu.make_async_remote_copy(
            src_ref=acc.at[pl.ds(to * tiles, tiles)], dst_ref=rbuf.at[k],
            send_sem=a_send.at[k], recv_sem=a_recv.at[k],
            device_id=(group, to * HEADS + head), device_id_type=MESH,
        )

    def finish(to):
        def one(t, c):
            b = to * tiles + t
            state = merge(load(acc, b), part(2, b))
            store(b, merge(state, part(3, b)))
            return c

        lax.fori_loop(0, tiles, one, 0)

    def finish_and_send(k, c):
        finish(lax.rem(quad + k, quads))
        a_copy(k).start()
        return c

    lax.fori_loop(1, quads, finish_and_send, 0)
    finish(quad)

    def wait_s(k, c):
        s_copy(k).wait_recv()
        return c

    lax.fori_loop(1, n, wait_s, 0)
    svt[...] = jnp.transpose(sbuf[1])
    keys = n * pad
    key_ids = lax.broadcasted_iota(jnp.int32, (keys, tile), 0)
    key_rows = (key_ids >> log2(pad)) * rows + (key_ids & (pad - 1))
    key_live = (key_ids & (pad - 1)) < rows
    lane_ids = lax.broadcasted_iota(jnp.int32, (keys, tile), 1)

    def span(t, c):
        b = quad * tiles + t
        ids = lane_ids + b * tile
        q_rows = (ids >> log2(block)) * rows + (ids & (rows - 1))
        visible = key_live & (key_rows >> log2(SPAN) == q_rows >> log2(SPAN)) & (key_rows <= q_rows)
        weights, top, total = weigh(dot_nt(sbuf[0], queries_of(b)), visible)
        store(b, merge(load(acc, b), (dot_nn(svt[...], weights), top, total)))
        return c

    lax.fori_loop(0, tiles, span, 0)

    def gather(k, c):
        a_copy(k).wait_recv()

        def one(t, c2):
            b = quad * tiles + t
            store(b, merge(load(acc, b), load(rbuf, k, t)))
            return c2

        lax.fori_loop(0, tiles, one, 0)
        return c

    lax.fori_loop(1, quads, gather, 0)

    def normal(t, c):
        num, top, total = load(acc, quad * tiles + t)
        obuf[pl.ds(pl.multiple_of(t * tile, tile), tile), :] = jnp.transpose(num / total).astype(BF16)
        return c

    lax.fori_loop(0, tiles, normal, 0)

    def o_copy(i):
        return pltpu.make_async_remote_copy(
            src_ref=obuf.at[pl.ds(pl.multiple_of(order[i] * block, block), block)], dst_ref=out.at[head],
            send_sem=o_send.at[i], recv_sem=o_recv.at[i],
            device_id=(group, quad * HEADS + order[i]), device_id_type=MESH,
        )

    for i in range(1, HEADS):
        o_copy(i).start()
    out[head] = obuf[pl.ds(pl.multiple_of(head * block, block), block), :]
    for i in range(1, HEADS):
        pltpu.make_async_remote_copy(
            src_ref=obuf.at[pl.ds(0, block)], dst_ref=out.at[order[i]],
            send_sem=o_send.at[i], recv_sem=o_recv.at[i],
            device_id=(group, quad * HEADS + order[i]), device_id_type=MESH,
        ).wait_recv()
    for i in range(1, HEADS):
        o_copy(i).wait_send()
        for copy in kv[i]:
            copy.wait_send()

    def drain(k, c):
        q_copy(k).wait_send()
        s_copy(k).wait_send()
        return c

    lax.fori_loop(1, n, drain, 0)

    def drain_a(k, c):
        a_copy(k).wait_send()
        return c

    lax.fori_loop(1, quads, drain_a, 0)


def shards(queries, span_keys, span_values, stored_keys, stored_values, shard_lens, span_starts):
    n = lax.axis_size("kvp")
    rows = queries.shape[0]
    slots = stored_keys.shape[0]
    pad = max(rows, 16)
    block = GROUP * rows
    quads = n // HEADS
    tile = min(256, HEADS * block)
    tiles = HEADS * block // tile
    ids = jnp.arange(n, dtype=jnp.int32)
    offsets = jnp.sum(jnp.where(ids[None, :] < ids[:, None], shard_lens[None, :], 0), axis=1)
    counts = jnp.minimum(shard_lens[:, None], span_starts[None, :] - offsets[:, None])
    q = queries.reshape(rows, QUERY_HEADS, HEAD_SIZE).transpose(1, 0, 2).reshape(HEADS, block, HEAD_SIZE)
    both = jnp.stack([span_keys, span_values]).reshape(2, rows, HEADS, HEAD_SIZE).transpose(2, 0, 1, 3)
    both = jnp.pad(both, ((0, 0), (0, 0), (0, pad - rows), (0, 0)))
    vmem = pl.BlockSpec(memory_space=pltpu.VMEM)
    dma = pltpu.SemaphoreType.DMA
    out = pl.pallas_call(
        functools.partial(kernel, n, rows, pad, tile),
        out_shape=jax.ShapeDtypeStruct((HEADS, block, HEAD_SIZE), BF16),
        in_specs=[
            pl.BlockSpec(memory_space=pltpu.SMEM), vmem, vmem,
            pl.BlockSpec(memory_space=pl.ANY), pl.BlockSpec(memory_space=pl.ANY),
        ],
        out_specs=vmem,
        scratch_shapes=[
            pltpu.VMEM((n * block, HEAD_SIZE), BF16),
            pltpu.VMEM((2, n * pad, HEAD_SIZE), BF16),
            pltpu.VMEM((HEADS, slots, HEAD_SIZE), BF16),
            pltpu.VMEM((HEADS, slots, HEAD_SIZE), BF16),
            pltpu.VMEM((HEADS, HEAD_SIZE, slots), BF16),
            pltpu.VMEM((HEAD_SIZE, n * pad), BF16),
            pltpu.VMEM((quads * tiles, HEAD_SIZE + 8, tile), F32),
            pltpu.VMEM((quads, tiles, HEAD_SIZE + 8, tile), F32),
            pltpu.VMEM((HEADS * block, HEAD_SIZE), BF16),
            dma((n,)), dma((n,)), dma((n,)), dma((n,)),
            dma((HEADS,)), dma((HEADS,)), dma((HEADS,)), dma((HEADS,)),
            dma((quads,)), dma((quads,)), dma((HEADS,)), dma((HEADS,)),
        ],
        compiler_params=pltpu.CompilerParams(
            collective_id=0, has_side_effects=True, vmem_limit_bytes=48 * 1024 * 1024
        ),
        name="spanned_attention",
    )(counts, q, both, stored_keys, stored_values)
    return out.reshape(QUERY_HEADS, rows, HEAD_SIZE).transpose(1, 0, 2).reshape(rows, QUERY_HEADS * HEAD_SIZE)


def solution(mesh):
    row = P(("groups", "kvp"), None)
    in_specs = (row, row, row, row, row, P("groups"), P("groups"))
    return jax.shard_map(shards, mesh=mesh, in_specs=in_specs, out_specs=row, check_vma=False)
```

```python
import functools

import jax
import jax.numpy as jnp
from jax import lax
from jax.experimental import pallas as pl
from jax.experimental.pallas import tpu as pltpu
from jax.sharding import PartitionSpec as P

QUERY_HEADS = 32
HEADS = 4
GROUP = QUERY_HEADS // HEADS
HEAD_SIZE = 128
SPAN = 128
SPANS = 2
NEG = -1e30
LEVELS = 32767.0
TINY = 1e-33
SCALE2 = HEAD_SIZE ** (-0.5) * 1.4426950408889634
F32 = jnp.float32
BF16 = jnp.bfloat16
MESH = pl.DeviceIdType.MESH


def log2(x):
    return x.bit_length() - 1


def weigh(scores, visible):
    masked = jnp.where(visible, scores, NEG)
    top = jnp.max(masked, axis=0, keepdims=True)
    weights = jnp.exp2(masked * SCALE2 - top * SCALE2)
    return weights.astype(BF16), top * SCALE2, jnp.sum(weights, axis=0, keepdims=True)


def dot_nt(a, b):
    return lax.dot_general(a, b, (((1,), (1,)), ((), ())), preferred_element_type=F32)


def dot_nn(a, b):
    return lax.dot_general(a, b, (((1,), (0,)), ((), ())), preferred_element_type=F32)


def merge(one, two):
    num1, top1, sum1 = one
    num2, top2, sum2 = two
    top = jnp.maximum(top1, top2)
    f1, f2 = jnp.exp2(top1 - top), jnp.exp2(top2 - top)
    return num1 * f1 + num2 * f2, top, sum1 * f1 + sum2 * f2


def kernel(
    n, rows, pad, tile,
    lens, starts, q_in, sk_in, sv_in, k_in, v_in, out,
    s_in, qbuf, sbuf, kbuf, vbuf, vt, svt, acc, coded, stats, rbuf, rstat, obuf,
    q_send, q_recv, s_send, s_recv, k_send, k_recv, v_send, v_recv, a_send, a_recv, t_send, t_recv, o_send, o_recv,
):
    group = lax.axis_index("groups")
    me = lax.axis_index("kvp")
    head = lax.rem(me, HEADS)
    quad = lax.div(me, HEADS)
    quads = n // HEADS
    block = GROUP * rows
    per_quad = HEADS * block
    tiles = per_quad // tile
    slots = kbuf.shape[1]

    barrier = pltpu.get_barrier_semaphore()
    for h in range(HEADS):
        for at, ref in enumerate((sk_in, sv_in)):
            s_in[h, at] = ref[:, h * HEAD_SIZE : (h + 1) * HEAD_SIZE]

    def greet(k, c):
        pl.semaphore_signal(barrier, inc=1, device_id=(group, lax.rem(me + k, n)), device_id_type=MESH)
        return c

    lax.fori_loop(1, n, greet, 0)
    pl.semaphore_wait(barrier, n - 1)

    def q_copy(k):
        to = lax.rem(me + k, n)
        return pltpu.make_async_remote_copy(
            src_ref=q_in.at[lax.rem(to, HEADS)],
            dst_ref=qbuf.at[pl.ds(pl.multiple_of(me * block, block), block)],
            send_sem=q_send.at[k], recv_sem=q_recv.at[k],
            device_id=(group, to), device_id_type=MESH,
        )

    def s_copy(k):
        to = lax.rem(me + k, n)
        return pltpu.make_async_remote_copy(
            src_ref=s_in.at[lax.rem(to, HEADS)],
            dst_ref=sbuf.at[:, pl.ds(pl.multiple_of(me * pad, pad), pad)],
            send_sem=s_send.at[k], recv_sem=s_recv.at[k],
            device_id=(group, to), device_id_type=MESH,
        )

    partner = head + 1 - 2 * lax.rem(head, 2)
    order = (head, partner, lax.rem(head + 2, HEADS), lax.rem(partner + 2, HEADS))

    def kv_copies(i):
        columns = pl.ds(pl.multiple_of(order[i] * HEAD_SIZE, HEAD_SIZE), HEAD_SIZE)
        if i == 0:
            return (
                pltpu.make_async_copy(k_in.at[:, columns], kbuf.at[0], k_recv.at[0]),
                pltpu.make_async_copy(v_in.at[:, columns], vbuf.at[0], v_recv.at[0]),
            )
        return tuple(
            pltpu.make_async_remote_copy(
                src_ref=src.at[:, columns], dst_ref=dst.at[i],
                send_sem=send.at[i], recv_sem=recv.at[i],
                device_id=(group, quad * HEADS + order[i]), device_id_type=MESH,
            )
            for src, dst, send, recv in ((k_in, kbuf, k_send, k_recv), (v_in, vbuf, v_send, v_recv))
        )

    kv = [kv_copies(i) for i in range(HEADS)]

    def send_q(k, c):
        q_copy(k).start()
        return c

    lax.fori_loop(1, n, send_q, 0)
    for i in range(HEADS):
        for copy in kv[i]:
            copy.start()

    def send_s(k, c):
        s_copy(k).start()
        return c

    lax.fori_loop(1, n, send_s, 0)
    qbuf[pl.ds(pl.multiple_of(me * block, block), block), :] = q_in[head]
    sbuf[:, pl.ds(pl.multiple_of(me * pad, pad), pad), :] = s_in[head]

    def wait_q(k, c):
        q_copy(k).wait_recv()
        return c

    lax.fori_loop(1, n, wait_q, 0)

    def wait_kv(i):
        for copy in kv[i]:
            if i == 0:
                copy.wait()
            else:
                copy.wait_recv()
        vt[i] = jnp.transpose(vbuf[i])

    def offset(j, totals):
        length = lens[j]
        return tuple(
            total + jnp.where(j < quad * HEADS + order[i], length, 0) for i, total in enumerate(totals)
        )

    offsets = lax.fori_loop(0, n, offset, (jnp.int32(0),) * HEADS)
    slot_ids = lax.broadcasted_iota(jnp.int32, (slots, tile), 0)
    stat_ids = lax.broadcasted_iota(jnp.int32, (8, tile), 0)

    def queries_of(b):
        return qbuf[pl.ds(pl.multiple_of(b * tile, tile), tile), :]

    def part(i, b):
        count = jnp.minimum(lens[quad * HEADS + order[i]], starts[lax.div(b * tile, GROUP * SPAN)] - offsets[i])
        weights, top, total = weigh(dot_nt(kbuf[i], queries_of(b)), slot_ids < count)
        return dot_nn(vt[i], weights), top, total

    def load(ref, *at):
        return (
            ref[(*at, slice(0, HEAD_SIZE))],
            ref[(*at, slice(HEAD_SIZE, HEAD_SIZE + 1))],
            ref[(*at, slice(HEAD_SIZE + 4, HEAD_SIZE + 5))],
        )

    def store(b, state):
        num, top, total = state
        acc[b, 0:HEAD_SIZE] = num
        acc[b, HEAD_SIZE : HEAD_SIZE + 8] = jnp.where(stat_ids < 4, top, total)

    wait_kv(0)

    def first(b, c):
        store(b, part(0, b))
        return c

    lax.fori_loop(0, quads * tiles, first, 0)
    wait_kv(1)

    def second(b, c):
        store(b, merge(load(acc, b), part(1, b)))
        return c

    lax.fori_loop(0, quads * tiles, second, 0)
    wait_kv(2)

    def third(b, c):
        store(b, merge(load(acc, b), part(2, b)))
        return c

    lax.fori_loop(0, quads * tiles, third, 0)
    wait_kv(3)

    def a_copies(k):
        to = lax.rem(quad + k, quads)
        return tuple(
            pltpu.make_async_remote_copy(
                src_ref=src.at[pl.ds(to * tiles, tiles)], dst_ref=dst.at[k],
                send_sem=send.at[k], recv_sem=recv.at[k],
                device_id=(group, to * HEADS + head), device_id_type=MESH,
            )
            for src, dst, send, recv in ((coded, rbuf, a_send, a_recv), (stats, rstat, t_send, t_recv))
        )

    def finish_and_send(k, c):
        def one(t, c2):
            b = lax.rem(quad + k, quads) * tiles + t
            num, top, total = merge(load(acc, b), part(3, b))
            level = jnp.maximum(jnp.max(jnp.abs(num), axis=0, keepdims=True), TINY)
            coded[b] = jnp.round(num * (LEVELS / level)).astype(jnp.int32).astype(jnp.int16)
            stats[b] = jnp.where(stat_ids < 2, top, jnp.where(stat_ids < 4, total, level * (1.0 / LEVELS)))
            return c2

        lax.fori_loop(0, tiles, one, 0)
        for copy in a_copies(k):
            copy.start()
        return c

    lax.fori_loop(1, quads, finish_and_send, 0)

    def finish(t, c):
        b = quad * tiles + t
        store(b, merge(load(acc, b), part(3, b)))
        return c

    lax.fori_loop(0, tiles, finish, 0)

    def wait_s(k, c):
        s_copy(k).wait_recv()
        return c

    lax.fori_loop(1, n, wait_s, 0)
    svt[...] = jnp.transpose(sbuf[1])
    keys = n * pad
    key_ids = lax.broadcasted_iota(jnp.int32, (keys, tile), 0)
    key_rows = (key_ids >> log2(pad)) * rows + (key_ids & (pad - 1))
    key_live = (key_ids & (pad - 1)) < rows
    lane_ids = lax.broadcasted_iota(jnp.int32, (keys, tile), 1)

    def span(t, c):
        b = quad * tiles + t
        ids = lane_ids + b * tile
        q_rows = (ids >> log2(block)) * rows + (ids & (rows - 1))
        visible = key_live & (key_rows >> log2(SPAN) == q_rows >> log2(SPAN)) & (key_rows <= q_rows)
        weights, top, total = weigh(dot_nt(sbuf[0], queries_of(b)), visible)
        store(b, merge(load(acc, b), (dot_nn(svt[...], weights), top, total)))
        return c

    lax.fori_loop(0, tiles, span, 0)

    def gather(k, c):
        for copy in a_copies(k):
            copy.wait_recv()

        def one(t, c2):
            b = quad * tiles + t
            num = rbuf[k, t].astype(jnp.int32).astype(F32) * rstat[k, t, 4:5]
            store(b, merge(load(acc, b), (num, rstat[k, t, 0:1], rstat[k, t, 2:3])))
            return c2

        lax.fori_loop(0, tiles, one, 0)
        return c

    lax.fori_loop(1, quads, gather, 0)

    def normal(t, c):
        num, top, total = load(acc, quad * tiles + t)
        obuf[pl.ds(pl.multiple_of(t * tile, tile), tile), :] = jnp.transpose(num / total).astype(BF16)
        return c

    lax.fori_loop(0, tiles, normal, 0)

    def o_copy(i):
        return pltpu.make_async_remote_copy(
            src_ref=obuf.at[pl.ds(pl.multiple_of(order[i] * block, block), block)], dst_ref=out.at[head],
            send_sem=o_send.at[i], recv_sem=o_recv.at[i],
            device_id=(group, quad * HEADS + order[i]), device_id_type=MESH,
        )

    for i in range(1, HEADS):
        o_copy(i).start()
    out[head] = obuf[pl.ds(pl.multiple_of(head * block, block), block), :]
    for i in range(1, HEADS):
        pltpu.make_async_remote_copy(
            src_ref=obuf.at[pl.ds(0, block)], dst_ref=out.at[order[i]],
            send_sem=o_send.at[i], recv_sem=o_recv.at[i],
            device_id=(group, quad * HEADS + order[i]), device_id_type=MESH,
        ).wait_recv()
    for i in range(1, HEADS):
        o_copy(i).wait_send()
        for copy in kv[i]:
            copy.wait_send()

    def drain(k, c):
        q_copy(k).wait_send()
        s_copy(k).wait_send()
        return c

    lax.fori_loop(1, n, drain, 0)

    def drain_a(k, c):
        for copy in a_copies(k):
            copy.wait_send()
        return c

    lax.fori_loop(1, quads, drain_a, 0)


def shards(queries, span_keys, span_values, stored_keys, stored_values, shard_lens, span_starts):
    n = lax.axis_size("kvp")
    rows = queries.shape[0]
    slots = stored_keys.shape[0]
    pad = max(rows, 16)
    block = GROUP * rows
    quads = n // HEADS
    tile = min(256, HEADS * block)
    tiles = HEADS * block // tile
    q = queries.reshape(rows, QUERY_HEADS, HEAD_SIZE).transpose(1, 0, 2).reshape(HEADS, block, HEAD_SIZE)
    span_keys, span_values = (
        jnp.pad(x, ((0, pad - rows), (0, 0))) if pad > rows else x for x in (span_keys, span_values)
    )
    vmem = pl.BlockSpec(memory_space=pltpu.VMEM)
    smem, hbm = pl.BlockSpec(memory_space=pltpu.SMEM), pl.BlockSpec(memory_space=pltpu.HBM)
    dma = pltpu.SemaphoreType.DMA
    out = pl.pallas_call(
        functools.partial(kernel, n, rows, pad, tile),
        out_shape=jax.ShapeDtypeStruct((HEADS, block, HEAD_SIZE), BF16),
        in_specs=[
            smem, smem, vmem, vmem, vmem, hbm, hbm,
        ],
        out_specs=vmem,
        scratch_shapes=[
            pltpu.VMEM((HEADS, 2, pad, HEAD_SIZE), BF16),
            pltpu.VMEM((n * block, HEAD_SIZE), BF16),
            pltpu.VMEM((2, n * pad, HEAD_SIZE), BF16),
            pltpu.VMEM((HEADS, slots, HEAD_SIZE), BF16),
            pltpu.VMEM((HEADS, slots, HEAD_SIZE), BF16),
            pltpu.VMEM((HEADS, HEAD_SIZE, slots), BF16),
            pltpu.VMEM((HEAD_SIZE, n * pad), BF16),
            pltpu.VMEM((quads * tiles, HEAD_SIZE + 8, tile), F32),
            pltpu.VMEM((quads * tiles, HEAD_SIZE, tile), jnp.int16),
            pltpu.VMEM((quads * tiles, 8, tile), F32),
            pltpu.VMEM((quads, tiles, HEAD_SIZE, tile), jnp.int16),
            pltpu.VMEM((quads, tiles, 8, tile), F32),
            pltpu.VMEM((HEADS * block, HEAD_SIZE), BF16),
            dma((n,)), dma((n,)), dma((n,)), dma((n,)),
            dma((HEADS,)), dma((HEADS,)), dma((HEADS,)), dma((HEADS,)),
            dma((quads,)), dma((quads,)), dma((quads,)), dma((quads,)), dma((HEADS,)), dma((HEADS,)),
        ],
        compiler_params=pltpu.CompilerParams(
            collective_id=0, has_side_effects=True, vmem_limit_bytes=48 * 1024 * 1024
        ),
        name="spanned_attention",
    )(shard_lens, span_starts, q, span_keys, span_values, stored_keys, stored_values)
    return out.reshape(QUERY_HEADS, rows, HEAD_SIZE).transpose(1, 0, 2).reshape(rows, QUERY_HEADS * HEAD_SIZE)


def solution(mesh):
    row = P(("groups", "kvp"), None)
    in_specs = (row, row, row, row, row, P("groups"), P("groups"))
    return jax.shard_map(shards, mesh=mesh, in_specs=in_specs, out_specs=row, check_vma=False)
```

```python
import functools

import jax
import jax.numpy as jnp
from jax import lax
from jax.experimental import pallas as pl
from jax.experimental.pallas import tpu as pltpu
from jax.sharding import PartitionSpec as P

QUERY_HEADS = 32
HEADS = 4
GROUP = QUERY_HEADS // HEADS
HEAD_SIZE = 128
SPAN = 128
SPANS = 2
NEG = -1e30
LEVELS = 32767.0
TINY = 1e-33
SCALE2 = HEAD_SIZE ** (-0.5) * 1.4426950408889634
F32 = jnp.float32
BF16 = jnp.bfloat16
MESH = pl.DeviceIdType.MESH


def log2(x):
    return x.bit_length() - 1


def weigh(scores, visible):
    masked = jnp.where(visible, scores, NEG)
    top = jnp.max(masked, axis=0, keepdims=True)
    weights = jnp.exp2(masked * SCALE2 - top * SCALE2)
    return weights.astype(BF16), top * SCALE2, jnp.sum(weights, axis=0, keepdims=True)


def dot_nt(a, b):
    return lax.dot_general(a, b, (((1,), (1,)), ((), ())), preferred_element_type=F32)


def dot_nn(a, b):
    return lax.dot_general(a, b, (((1,), (0,)), ((), ())), preferred_element_type=F32)


def merge(one, two):
    num1, top1, sum1 = one
    num2, top2, sum2 = two
    top = jnp.maximum(top1, top2)
    f1, f2 = jnp.exp2(top1 - top), jnp.exp2(top2 - top)
    return num1 * f1 + num2 * f2, top, sum1 * f1 + sum2 * f2


def kernel(
    n, rows, pad, tile,
    lens, starts, q_in, sk_in, sv_in, k_in, v_in, out,
    s_in, qbuf, sbuf, kbuf, vbuf, vt, svt, acc, coded, stats, rbuf, rstat, obuf,
    q_send, q_recv, s_send, s_recv, k_send, k_recv, v_send, v_recv, a_send, a_recv, t_send, t_recv, o_send, o_recv,
):
    group = lax.axis_index("groups")
    me = lax.axis_index("kvp")
    head = lax.rem(me, HEADS)
    quad = lax.div(me, HEADS)
    quads = n // HEADS
    block = GROUP * rows
    per_quad = HEADS * block
    tiles = per_quad // tile
    slots = kbuf.shape[1]

    barrier = pltpu.get_barrier_semaphore()
    for h in range(HEADS):
        for at, ref in enumerate((sk_in, sv_in)):
            s_in[h, at] = ref[:, h * HEAD_SIZE : (h + 1) * HEAD_SIZE]

    def greet(k, c):
        pl.semaphore_signal(barrier, inc=1, device_id=(group, lax.rem(me + k, n)), device_id_type=MESH)
        return c

    lax.fori_loop(1, n, greet, 0)
    pl.semaphore_wait(barrier, n - 1)

    def q_copy(k):
        to = lax.rem(me + k, n)
        return pltpu.make_async_remote_copy(
            src_ref=q_in.at[lax.rem(to, HEADS)],
            dst_ref=qbuf.at[pl.ds(pl.multiple_of(me * block, block), block)],
            send_sem=q_send.at[k], recv_sem=q_recv.at[k],
            device_id=(group, to), device_id_type=MESH,
        )

    def s_copy(k):
        to = lax.rem(me + k, n)
        return pltpu.make_async_remote_copy(
            src_ref=s_in.at[lax.rem(to, HEADS)],
            dst_ref=sbuf.at[:, pl.ds(pl.multiple_of(me * pad, pad), pad)],
            send_sem=s_send.at[k], recv_sem=s_recv.at[k],
            device_id=(group, to), device_id_type=MESH,
        )

    partner = head + 1 - 2 * lax.rem(head, 2)
    order = (head, partner, lax.rem(head + 2, HEADS), lax.rem(partner + 2, HEADS))

    def kv_copies(i):
        columns = pl.ds(pl.multiple_of(order[i] * HEAD_SIZE, HEAD_SIZE), HEAD_SIZE)
        if i == 0:
            return (
                pltpu.make_async_copy(k_in.at[:, columns], kbuf.at[0], k_recv.at[0]),
                pltpu.make_async_copy(v_in.at[:, columns], vbuf.at[0], v_recv.at[0]),
            )
        return tuple(
            pltpu.make_async_remote_copy(
                src_ref=src.at[:, columns], dst_ref=dst.at[i],
                send_sem=send.at[i], recv_sem=recv.at[i],
                device_id=(group, quad * HEADS + order[i]), device_id_type=MESH,
            )
            for src, dst, send, recv in ((k_in, kbuf, k_send, k_recv), (v_in, vbuf, v_send, v_recv))
        )

    kv = [kv_copies(i) for i in range(HEADS)]

    def send_q(k, c):
        q_copy(k).start()
        return c

    lax.fori_loop(1, n, send_q, 0)
    for i in range(HEADS):
        for copy in kv[i]:
            copy.start()

    def send_s(k, c):
        s_copy(k).start()
        return c

    lax.fori_loop(1, n, send_s, 0)
    qbuf[pl.ds(pl.multiple_of(me * block, block), block), :] = q_in[head]
    sbuf[:, pl.ds(pl.multiple_of(me * pad, pad), pad), :] = s_in[head]

    def wait_q(b):
        for j in range(tile // block):
            k = lax.rem(me + n - (b * (tile // block) + j), n)

            @pl.when(k > 0)
            def _():
                q_copy(k).wait_recv()

    def wait_kv(i):
        for copy in kv[i]:
            if i == 0:
                copy.wait()
            else:
                copy.wait_recv()
        vt[i] = jnp.transpose(vbuf[i])

    def offset(j, totals):
        length = lens[j]
        return tuple(
            total + jnp.where(j < quad * HEADS + order[i], length, 0) for i, total in enumerate(totals)
        )

    offsets = lax.fori_loop(0, n, offset, (jnp.int32(0),) * HEADS)
    slot_ids = lax.broadcasted_iota(jnp.int32, (slots, tile), 0)
    stat_ids = lax.broadcasted_iota(jnp.int32, (8, tile), 0)

    def queries_of(b):
        return qbuf[pl.ds(pl.multiple_of(b * tile, tile), tile), :]

    def part(i, b):
        count = jnp.minimum(lens[quad * HEADS + order[i]], starts[lax.div(b * tile, GROUP * SPAN)] - offsets[i])
        weights, top, total = weigh(dot_nt(kbuf[i], queries_of(b)), slot_ids < count)
        return dot_nn(vt[i], weights), top, total

    def load(ref, *at):
        return (
            ref[(*at, slice(0, HEAD_SIZE))],
            ref[(*at, slice(HEAD_SIZE, HEAD_SIZE + 1))],
            ref[(*at, slice(HEAD_SIZE + 4, HEAD_SIZE + 5))],
        )

    def store(b, state):
        num, top, total = state
        acc[b, 0:HEAD_SIZE] = num
        acc[b, HEAD_SIZE : HEAD_SIZE + 8] = jnp.where(stat_ids < 4, top, total)

    wait_kv(0)
    wait_kv(1)

    def first(u, c):
        b = lax.rem(quad * tiles + u, quads * tiles)
        wait_q(b)
        store(b, merge(part(0, b), part(1, b)))
        return c

    lax.fori_loop(0, quads * tiles, first, 0)
    wait_kv(2)

    def third(b, c):
        store(b, merge(load(acc, b), part(2, b)))
        return c

    lax.fori_loop(0, quads * tiles, third, 0, unroll=2)
    wait_kv(3)

    def a_copies(k):
        to = lax.rem(quad + k, quads)
        return tuple(
            pltpu.make_async_remote_copy(
                src_ref=src.at[pl.ds(to * tiles, tiles)], dst_ref=dst.at[k],
                send_sem=send.at[k], recv_sem=recv.at[k],
                device_id=(group, to * HEADS + head), device_id_type=MESH,
            )
            for src, dst, send, recv in ((coded, rbuf, a_send, a_recv), (stats, rstat, t_send, t_recv))
        )

    def finish_and_send(k, c):
        def one(t, c2):
            b = lax.rem(quad + k, quads) * tiles + t
            num, top, total = merge(load(acc, b), part(3, b))
            level = jnp.maximum(jnp.max(jnp.abs(num), axis=0, keepdims=True), TINY)
            coded[b] = jnp.round(num * (LEVELS / level)).astype(jnp.int32).astype(jnp.int16)
            stats[b] = jnp.where(stat_ids < 2, top, jnp.where(stat_ids < 4, total, level * (1.0 / LEVELS)))
            return c2

        lax.fori_loop(0, tiles, one, 0, unroll=tiles)
        for copy in a_copies(k):
            copy.start()
        return c

    lax.fori_loop(1, quads, finish_and_send, 0)

    def finish(t, c):
        b = quad * tiles + t
        store(b, merge(load(acc, b), part(3, b)))
        return c

    lax.fori_loop(0, tiles, finish, 0, unroll=tiles)

    def wait_s(k, c):
        s_copy(k).wait_recv()
        return c

    lax.fori_loop(1, n, wait_s, 0)
    svt[...] = jnp.transpose(sbuf[1])
    keys = n * pad
    key_ids = lax.broadcasted_iota(jnp.int32, (keys, tile), 0)
    key_rows = (key_ids >> log2(pad)) * rows + (key_ids & (pad - 1))
    key_live = (key_ids & (pad - 1)) < rows
    lane_ids = lax.broadcasted_iota(jnp.int32, (keys, tile), 1)

    def span(t, c):
        b = quad * tiles + t
        ids = lane_ids + b * tile
        q_rows = (ids >> log2(block)) * rows + (ids & (rows - 1))
        visible = key_live & (key_rows >> log2(SPAN) == q_rows >> log2(SPAN)) & (key_rows <= q_rows)
        weights, top, total = weigh(dot_nt(sbuf[0], queries_of(b)), visible)
        store(b, merge(load(acc, b), (dot_nn(svt[...], weights), top, total)))
        return c

    lax.fori_loop(0, tiles, span, 0, unroll=tiles)

    def gather(k, c):
        for copy in a_copies(k):
            copy.wait_recv()

        def one(t, c2):
            b = quad * tiles + t
            num = rbuf[k, t].astype(jnp.int32).astype(F32) * rstat[k, t, 4:5]
            store(b, merge(load(acc, b), (num, rstat[k, t, 0:1], rstat[k, t, 2:3])))
            return c2

        lax.fori_loop(0, tiles, one, 0)
        return c

    lax.fori_loop(1, quads, gather, 0)

    def normal(t, c):
        num, top, total = load(acc, quad * tiles + t)
        obuf[pl.ds(pl.multiple_of(t * tile, tile), tile), :] = jnp.transpose(num / total).astype(BF16)
        return c

    lax.fori_loop(0, tiles, normal, 0, unroll=tiles)

    def o_copy(i):
        return pltpu.make_async_remote_copy(
            src_ref=obuf.at[pl.ds(pl.multiple_of(order[i] * block, block), block)], dst_ref=out.at[head],
            send_sem=o_send.at[i], recv_sem=o_recv.at[i],
            device_id=(group, quad * HEADS + order[i]), device_id_type=MESH,
        )

    for i in range(1, HEADS):
        o_copy(i).start()
    out[head] = obuf[pl.ds(pl.multiple_of(head * block, block), block), :]
    for i in range(1, HEADS):
        pltpu.make_async_remote_copy(
            src_ref=obuf.at[pl.ds(0, block)], dst_ref=out.at[order[i]],
            send_sem=o_send.at[i], recv_sem=o_recv.at[i],
            device_id=(group, quad * HEADS + order[i]), device_id_type=MESH,
        ).wait_recv()
    for i in range(1, HEADS):
        o_copy(i).wait_send()
        for copy in kv[i]:
            copy.wait_send()

    def drain(k, c):
        q_copy(k).wait_send()
        s_copy(k).wait_send()
        return c

    lax.fori_loop(1, n, drain, 0)

    def drain_a(k, c):
        for copy in a_copies(k):
            copy.wait_send()
        return c

    lax.fori_loop(1, quads, drain_a, 0)


def shards(queries, span_keys, span_values, stored_keys, stored_values, shard_lens, span_starts):
    n = lax.axis_size("kvp")
    rows = queries.shape[0]
    slots = stored_keys.shape[0]
    pad = max(rows, 16)
    block = GROUP * rows
    quads = n // HEADS
    tile = min(512, HEADS * block)
    tiles = HEADS * block // tile
    q = queries.reshape(rows, QUERY_HEADS, HEAD_SIZE).transpose(1, 0, 2).reshape(HEADS, block, HEAD_SIZE)
    span_keys, span_values = (
        jnp.pad(x, ((0, pad - rows), (0, 0))) if pad > rows else x for x in (span_keys, span_values)
    )
    vmem = pl.BlockSpec(memory_space=pltpu.VMEM)
    smem, hbm = pl.BlockSpec(memory_space=pltpu.SMEM), pl.BlockSpec(memory_space=pltpu.HBM)
    dma = pltpu.SemaphoreType.DMA
    out = pl.pallas_call(
        functools.partial(kernel, n, rows, pad, tile),
        out_shape=jax.ShapeDtypeStruct((HEADS, block, HEAD_SIZE), BF16),
        in_specs=[
            smem, smem, vmem, vmem, vmem, hbm, hbm,
        ],
        out_specs=vmem,
        scratch_shapes=[
            pltpu.VMEM((HEADS, 2, pad, HEAD_SIZE), BF16),
            pltpu.VMEM((n * block, HEAD_SIZE), BF16),
            pltpu.VMEM((2, n * pad, HEAD_SIZE), BF16),
            pltpu.VMEM((HEADS, slots, HEAD_SIZE), BF16),
            pltpu.VMEM((HEADS, slots, HEAD_SIZE), BF16),
            pltpu.VMEM((HEADS, HEAD_SIZE, slots), BF16),
            pltpu.VMEM((HEAD_SIZE, n * pad), BF16),
            pltpu.VMEM((quads * tiles, HEAD_SIZE + 8, tile), F32),
            pltpu.VMEM((quads * tiles, HEAD_SIZE, tile), jnp.int16),
            pltpu.VMEM((quads * tiles, 8, tile), F32),
            pltpu.VMEM((quads, tiles, HEAD_SIZE, tile), jnp.int16),
            pltpu.VMEM((quads, tiles, 8, tile), F32),
            pltpu.VMEM((HEADS * block, HEAD_SIZE), BF16),
            dma((n,)), dma((n,)), dma((n,)), dma((n,)),
            dma((HEADS,)), dma((HEADS,)), dma((HEADS,)), dma((HEADS,)),
            dma((quads,)), dma((quads,)), dma((quads,)), dma((quads,)), dma((HEADS,)), dma((HEADS,)),
        ],
        compiler_params=pltpu.CompilerParams(
            collective_id=0, has_side_effects=True, vmem_limit_bytes=62 * 1024 * 1024
        ),
        name="spanned_attention",
    )(shard_lens, span_starts, q, span_keys, span_values, stored_keys, stored_values)
    return out.reshape(QUERY_HEADS, rows, HEAD_SIZE).transpose(1, 0, 2).reshape(rows, QUERY_HEADS * HEAD_SIZE)


def solution(mesh):
    row = P(("groups", "kvp"), None)
    in_specs = (row, row, row, row, row, P("groups"), P("groups"))
    return jax.shard_map(shards, mesh=mesh, in_specs=in_specs, out_specs=row, check_vma=False)
```

```python
import functools

import jax
import jax.numpy as jnp
from jax import lax
from jax.experimental import pallas as pl
from jax.experimental.pallas import tpu as pltpu
from jax.sharding import PartitionSpec as P

QUERY_HEADS = 32
HEADS = 4
GROUP = QUERY_HEADS // HEADS
HEAD_SIZE = 128
SPAN = 128
SPANS = 2
NEG = -1e30
LEVELS = 32767.0
TINY = 1e-33
SCALE2 = HEAD_SIZE ** (-0.5) * 1.4426950408889634
F32 = jnp.float32
BF16 = jnp.bfloat16
MESH = pl.DeviceIdType.MESH


def log2(x):
    return x.bit_length() - 1


def weigh(masked):
    top = jnp.max(masked, axis=0, keepdims=True)
    weights = jnp.exp2(masked * SCALE2 - top * SCALE2)
    return weights.astype(BF16), top * SCALE2, jnp.sum(weights, axis=0, keepdims=True)


def dot_nt(a, b):
    return lax.dot_general(a, b, (((1,), (1,)), ((), ())), preferred_element_type=F32)


def dot_nn(a, b):
    return lax.dot_general(a, b, (((1,), (0,)), ((), ())), preferred_element_type=F32)


def merge(one, two):
    num1, top1, sum1 = one
    num2, top2, sum2 = two
    top = jnp.maximum(top1, top2)
    f1, f2 = jnp.exp2(top1 - top), jnp.exp2(top2 - top)
    return num1 * f1 + num2 * f2, top, sum1 * f1 + sum2 * f2


def kernel(
    n, rows, pad, tile,
    lens, starts, q_in, sk_in, sv_in, k_in, v_in, out,
    s_in, qbuf, sbuf, kbuf, vbuf, vt, svt, acc, coded, stats, rbuf, rstat, obuf,
    q_send, q_recv, s_send, s_recv, k_send, k_recv, v_send, v_recv, a_send, a_recv, t_send, t_recv, o_send, o_recv,
):
    group = lax.axis_index("groups")
    me = lax.axis_index("kvp")
    head = lax.rem(me, HEADS)
    quad = lax.div(me, HEADS)
    quads = n // HEADS
    block = GROUP * rows
    per_quad = HEADS * block
    tiles = per_quad // tile
    slots = kbuf.shape[1]

    barrier = pltpu.get_barrier_semaphore()
    for h in range(HEADS):
        for at, ref in enumerate((sk_in, sv_in)):
            s_in[h, at] = ref[:, h * HEAD_SIZE : (h + 1) * HEAD_SIZE]

    def greet(k, c):
        pl.semaphore_signal(barrier, inc=1, device_id=(group, lax.rem(me + k, n)), device_id_type=MESH)
        return c

    lax.fori_loop(1, n, greet, 0)
    pl.semaphore_wait(barrier, n - 1)

    def q_copy(k):
        to = lax.rem(me + k, n)
        return pltpu.make_async_remote_copy(
            src_ref=q_in.at[lax.rem(to, HEADS)],
            dst_ref=qbuf.at[pl.ds(pl.multiple_of(me * block, block), block)],
            send_sem=q_send.at[k], recv_sem=q_recv.at[k],
            device_id=(group, to), device_id_type=MESH,
        )

    def s_copy(k):
        to = lax.rem(me + k, n)
        return pltpu.make_async_remote_copy(
            src_ref=s_in.at[lax.rem(to, HEADS)],
            dst_ref=sbuf.at[:, pl.ds(pl.multiple_of(me * pad, pad), pad)],
            send_sem=s_send.at[k], recv_sem=s_recv.at[k],
            device_id=(group, to), device_id_type=MESH,
        )

    partner = head + 1 - 2 * lax.rem(head, 2)
    order = (head, partner, lax.rem(head + 2, HEADS), lax.rem(partner + 2, HEADS))

    def kv_copies(i):
        columns = pl.ds(pl.multiple_of(order[i] * HEAD_SIZE, HEAD_SIZE), HEAD_SIZE)
        if i == 0:
            return (
                pltpu.make_async_copy(k_in.at[:, columns], kbuf.at[0], k_recv.at[0]),
                pltpu.make_async_copy(v_in.at[:, columns], vbuf.at[0], v_recv.at[0]),
            )
        return tuple(
            pltpu.make_async_remote_copy(
                src_ref=src.at[:, columns], dst_ref=dst.at[i],
                send_sem=send.at[i], recv_sem=recv.at[i],
                device_id=(group, quad * HEADS + order[i]), device_id_type=MESH,
            )
            for src, dst, send, recv in ((k_in, kbuf, k_send, k_recv), (v_in, vbuf, v_send, v_recv))
        )

    kv = [kv_copies(i) for i in range(HEADS)]

    def send_q(k, c):
        q_copy(k).start()
        return c

    lax.fori_loop(1, n, send_q, 0)
    for i in range(HEADS):
        for copy in kv[i]:
            copy.start()

    def send_s(k, c):
        s_copy(k).start()
        return c

    lax.fori_loop(1, n, send_s, 0)
    qbuf[pl.ds(pl.multiple_of(me * block, block), block), :] = q_in[head]
    sbuf[:, pl.ds(pl.multiple_of(me * pad, pad), pad), :] = s_in[head]

    def wait_q(b):
        for j in range(tile // block):
            k = lax.rem(me + n - (b * (tile // block) + j), n)

            @pl.when(k > 0)
            def _():
                q_copy(k).wait_recv()

    def wait_kv(i):
        for copy in kv[i]:
            if i == 0:
                copy.wait()
            else:
                copy.wait_recv()
        vt[i] = jnp.transpose(vbuf[i])

    def offset(j, totals):
        length = lens[j]
        return tuple(
            total + jnp.where(j < quad * HEADS + order[i], length, 0) for i, total in enumerate(totals)
        )

    offsets = lax.fori_loop(0, n, offset, (jnp.int32(0),) * HEADS)
    lanes = min(tile, 128)
    slot_ids = lax.broadcasted_iota(jnp.int32, (slots, lanes), 0)
    stat_ids = lax.broadcasted_iota(jnp.int32, (8, tile), 0)

    def queries_of(b):
        return qbuf[pl.ds(pl.multiple_of(b * tile, tile), tile), :]

    def part(i, b):
        count = jnp.minimum(lens[quad * HEADS + order[i]], starts[lax.div(b * tile, GROUP * SPAN)] - offsets[i])
        bias = jnp.where(slot_ids < count, 0.0, NEG).astype(F32)
        weights, top, total = weigh(dot_nt(kbuf[i], queries_of(b)) + jnp.concatenate([bias] * (tile // lanes), axis=1))
        return dot_nn(vt[i], weights), top, total

    def load(ref, *at):
        return (
            ref[(*at, slice(0, HEAD_SIZE))],
            ref[(*at, slice(HEAD_SIZE, HEAD_SIZE + 1))],
            ref[(*at, slice(HEAD_SIZE + 4, HEAD_SIZE + 5))],
        )

    def store(b, state):
        num, top, total = state
        acc[b, 0:HEAD_SIZE] = num
        acc[b, HEAD_SIZE : HEAD_SIZE + 8] = jnp.where(stat_ids < 4, top, total)

    wait_kv(0)
    wait_kv(1)

    def first(u, c):
        b = lax.rem(quad * tiles + u, quads * tiles)
        wait_q(b)
        store(b, merge(part(0, b), part(1, b)))
        return c

    lax.fori_loop(0, quads * tiles, first, 0)
    wait_kv(2)

    def third(b, c):
        store(b, merge(load(acc, b), part(2, b)))
        return c

    lax.fori_loop(0, quads * tiles, third, 0, unroll=2)
    wait_kv(3)

    def a_copies(k):
        to = lax.rem(quad + k, quads)
        return tuple(
            pltpu.make_async_remote_copy(
                src_ref=src.at[pl.ds(to * tiles, tiles)], dst_ref=dst.at[k],
                send_sem=send.at[k], recv_sem=recv.at[k],
                device_id=(group, to * HEADS + head), device_id_type=MESH,
            )
            for src, dst, send, recv in ((coded, rbuf, a_send, a_recv), (stats, rstat, t_send, t_recv))
        )

    def finish_and_send(k, c):
        def one(t, c2):
            b = lax.rem(quad + k, quads) * tiles + t
            num, top, total = merge(load(acc, b), part(3, b))
            level = jnp.maximum(jnp.max(jnp.abs(num), axis=0, keepdims=True), TINY)
            coded[b] = jnp.round(num * (LEVELS / level)).astype(jnp.int32).astype(jnp.int16)
            stats[b] = jnp.where(stat_ids < 2, top, jnp.where(stat_ids < 4, total, level * (1.0 / LEVELS)))
            return c2

        lax.fori_loop(0, tiles, one, 0, unroll=tiles)
        for copy in a_copies(k):
            copy.start()
        return c

    lax.fori_loop(1, quads, finish_and_send, 0)

    def finish(t, c):
        b = quad * tiles + t
        store(b, merge(load(acc, b), part(3, b)))
        return c

    lax.fori_loop(0, tiles, finish, 0, unroll=tiles)

    def wait_s(k, c):
        s_copy(k).wait_recv()
        return c

    lax.fori_loop(1, n, wait_s, 0)
    svt[...] = jnp.transpose(sbuf[1])
    keys = n * pad
    key_ids = lax.broadcasted_iota(jnp.int32, (keys, tile), 0)
    key_rows = (key_ids >> log2(pad)) * rows + (key_ids & (pad - 1))
    key_live = (key_ids & (pad - 1)) < rows
    lane_ids = lax.broadcasted_iota(jnp.int32, (keys, tile), 1)

    def span(t, c):
        b = quad * tiles + t
        ids = lane_ids + b * tile
        q_rows = (ids >> log2(block)) * rows + (ids & (rows - 1))
        visible = key_live & (key_rows >> log2(SPAN) == q_rows >> log2(SPAN)) & (key_rows <= q_rows)
        weights, top, total = weigh(jnp.where(visible, dot_nt(sbuf[0], queries_of(b)), NEG))
        store(b, merge(load(acc, b), (dot_nn(svt[...], weights), top, total)))
        return c

    lax.fori_loop(0, tiles, span, 0, unroll=tiles)

    def gather(k, c):
        for copy in a_copies(k):
            copy.wait_recv()

        def one(t, c2):
            b = quad * tiles + t
            num = rbuf[k, t].astype(jnp.int32).astype(F32) * rstat[k, t, 4:5]
            store(b, merge(load(acc, b), (num, rstat[k, t, 0:1], rstat[k, t, 2:3])))
            return c2

        lax.fori_loop(0, tiles, one, 0)
        return c

    lax.fori_loop(1, quads, gather, 0)

    def normal(t, c):
        num, top, total = load(acc, quad * tiles + t)
        obuf[pl.ds(pl.multiple_of(t * tile, tile), tile), :] = jnp.transpose(num / total).astype(BF16)
        return c

    lax.fori_loop(0, tiles, normal, 0, unroll=tiles)

    def o_copy(i):
        return pltpu.make_async_remote_copy(
            src_ref=obuf.at[pl.ds(pl.multiple_of(order[i] * block, block), block)], dst_ref=out.at[head],
            send_sem=o_send.at[i], recv_sem=o_recv.at[i],
            device_id=(group, quad * HEADS + order[i]), device_id_type=MESH,
        )

    for i in range(1, HEADS):
        o_copy(i).start()
    out[head] = obuf[pl.ds(pl.multiple_of(head * block, block), block), :]
    for i in range(1, HEADS):
        pltpu.make_async_remote_copy(
            src_ref=obuf.at[pl.ds(0, block)], dst_ref=out.at[order[i]],
            send_sem=o_send.at[i], recv_sem=o_recv.at[i],
            device_id=(group, quad * HEADS + order[i]), device_id_type=MESH,
        ).wait_recv()
    for i in range(1, HEADS):
        o_copy(i).wait_send()
        for copy in kv[i]:
            copy.wait_send()

    def drain(k, c):
        q_copy(k).wait_send()
        s_copy(k).wait_send()
        return c

    lax.fori_loop(1, n, drain, 0)

    def drain_a(k, c):
        for copy in a_copies(k):
            copy.wait_send()
        return c

    lax.fori_loop(1, quads, drain_a, 0)


def shards(queries, span_keys, span_values, stored_keys, stored_values, shard_lens, span_starts):
    n = lax.axis_size("kvp")
    rows = queries.shape[0]
    slots = stored_keys.shape[0]
    pad = max(rows, 16)
    block = GROUP * rows
    quads = n // HEADS
    tile = min(512, HEADS * block)
    tiles = HEADS * block // tile
    q = queries.reshape(rows, QUERY_HEADS, HEAD_SIZE).transpose(1, 0, 2).reshape(HEADS, block, HEAD_SIZE)
    span_keys, span_values = (
        jnp.pad(x, ((0, pad - rows), (0, 0))) if pad > rows else x for x in (span_keys, span_values)
    )
    vmem = pl.BlockSpec(memory_space=pltpu.VMEM)
    smem, hbm = pl.BlockSpec(memory_space=pltpu.SMEM), pl.BlockSpec(memory_space=pltpu.HBM)
    dma = pltpu.SemaphoreType.DMA
    out = pl.pallas_call(
        functools.partial(kernel, n, rows, pad, tile),
        out_shape=jax.ShapeDtypeStruct((HEADS, block, HEAD_SIZE), BF16),
        in_specs=[
            smem, smem, vmem, vmem, vmem, hbm, hbm,
        ],
        out_specs=vmem,
        scratch_shapes=[
            pltpu.VMEM((HEADS, 2, pad, HEAD_SIZE), BF16),
            pltpu.VMEM((n * block, HEAD_SIZE), BF16),
            pltpu.VMEM((2, n * pad, HEAD_SIZE), BF16),
            pltpu.VMEM((HEADS, slots, HEAD_SIZE), BF16),
            pltpu.VMEM((HEADS, slots, HEAD_SIZE), BF16),
            pltpu.VMEM((HEADS, HEAD_SIZE, slots), BF16),
            pltpu.VMEM((HEAD_SIZE, n * pad), BF16),
            pltpu.VMEM((quads * tiles, HEAD_SIZE + 8, tile), F32),
            pltpu.VMEM((quads * tiles, HEAD_SIZE, tile), jnp.int16),
            pltpu.VMEM((quads * tiles, 8, tile), F32),
            pltpu.VMEM((quads, tiles, HEAD_SIZE, tile), jnp.int16),
            pltpu.VMEM((quads, tiles, 8, tile), F32),
            pltpu.VMEM((HEADS * block, HEAD_SIZE), BF16),
            dma((n,)), dma((n,)), dma((n,)), dma((n,)),
            dma((HEADS,)), dma((HEADS,)), dma((HEADS,)), dma((HEADS,)),
            dma((quads,)), dma((quads,)), dma((quads,)), dma((quads,)), dma((HEADS,)), dma((HEADS,)),
        ],
        compiler_params=pltpu.CompilerParams(
            collective_id=0, has_side_effects=True, vmem_limit_bytes=62 * 1024 * 1024
        ),
        name="spanned_attention",
    )(shard_lens, span_starts, q, span_keys, span_values, stored_keys, stored_values)
    return out.reshape(QUERY_HEADS, rows, HEAD_SIZE).transpose(1, 0, 2).reshape(rows, QUERY_HEADS * HEAD_SIZE)


def solution(mesh):
    row = P(("groups", "kvp"), None)
    in_specs = (row, row, row, row, row, P("groups"), P("groups"))
    return jax.shard_map(shards, mesh=mesh, in_specs=in_specs, out_specs=row, check_vma=False)
```
